32 devices in a mesh: segment: 4 (over z), row: 4 (over y, x), col: 2 (over core).
Axes of the slice: x: 2, y: 2, z: 4, core: 2. Of those that a mesh axis runs over, the one named last changes fastest.
Arguments:
- weights: bfloat16 [4, 4096, 4096], P('segment', 'row', 'col'), may hold values from -0.09375 to 0.09375
- layer_gains: float32 [4, 4096], P('segment', 'col'), may hold values from -0.5 to 0.5
- incoming: bfloat16 [4, 256, 4096], P('segment', 'row', 'col'), may hold values from -6 to 6
- fresh_batch: bfloat16 [256, 4096], P('row', 'col'), may hold values from -6 to 6
- returning: bfloat16 [4, 256, 4096], P('segment', 'row', 'col'), may hold values from -6 to 6
- fresh_cotangent: bfloat16 [256, 4096], P('row', 'col'), may hold values from -6 to 6
- stashed_inputs: bfloat16 [4, 2, 256, 4096], P('segment', None, 'row', 'col'), may hold values from -6 to 6
Outputs:
- layer_outputs: bfloat16 [4, 2, 256, 4096], P('segment', None, 'row', 'col')
- input_grads: bfloat16 [4, 2, 256, 4096], P('segment', None, 'row', 'col')
The draws below stay inside these ranges and needn't reach their ends.
All inputs are finite; a program needn't handle non-finite values.
Results may differ from the reference program's by a relative error of at most 0.0055.
Values may be sent and summed in bfloat16 or wider, within the bound.
No kernel may reach another device: no remote copies, remote signals or barrier semaphores. Data moves between devices by JAX's collectives and lax.ppermute only.
A program may use at most 64 MiB of HBM per device.

```python
import jax
import jax.numpy as jnp
from jax import lax

D = 4096
TOKENS_MB = 256
SEGMENTS = 4


def block_scale(key, shape, split, least, high):
    gain = 1.0
    for axis_at, parts in split:
        draws = jax.random.uniform(jax.random.fold_in(jax.random.fold_in(key, 6), axis_at), (parts,), jnp.float32, least / len(split), high / len(split))
        gain = gain * jnp.repeat(jnp.exp(draws), shape[axis_at] // parts).reshape((-1,) + (1,) * (len(shape) - 1 - axis_at))
    return gain


def scatter_about(stream_key, dims, deviation, limit, split=(), dtype=jnp.bfloat16):
    level = block_scale(stream_key, dims, split, -0.22, 0.18) if split else 1.0
    drawn = jax.random.normal(stream_key, dims, jnp.float32) * deviation * level
    return jnp.minimum(jnp.maximum(drawn, -limit), limit).astype(dtype)


def setup_inputs(seed: int = 0) -> dict:
    arg_keys = jax.random.split(jax.random.key(seed), 8)
    weights = scatter_about(arg_keys[0], (SEGMENTS, D, D), D ** -0.5, 0.09375, ((0, 4), (1, 4), (2, 2)))
    layer_gains = jnp.clip(jax.random.uniform(arg_keys[1], (SEGMENTS, D), jnp.float32, -0.5, 0.5) * block_scale(arg_keys[1], (SEGMENTS, D), ((0, 4), (1, 2)), -0.4, 0.0), -0.5, 0.5)
    incoming = scatter_about(arg_keys[2], (SEGMENTS, TOKENS_MB, D), 1.0, 6.0, ((0, 4), (1, 4), (2, 2)))
    fresh_batch = scatter_about(arg_keys[3], (TOKENS_MB, D), 1.0, 6.0, ((0, 4), (1, 2)))
    returning = scatter_about(arg_keys[4], (SEGMENTS, TOKENS_MB, D), 1.0, 6.0, ((0, 4), (1, 4), (2, 2)))
    fresh_cotangent = scatter_about(arg_keys[5], (TOKENS_MB, D), 1.0, 6.0, ((0, 4), (1, 2)))
    stashed_inputs = scatter_about(arg_keys[6], (SEGMENTS, 2, TOKENS_MB, D), 1.0, 6.0, ((0, 4), (2, 4), (3, 2)))
    return {"weights": weights, "layer_gains": layer_gains, "incoming": incoming, "fresh_batch": fresh_batch, "returning": returning, "fresh_cotangent": fresh_cotangent, "stashed_inputs": stashed_inputs}


def silu_slope(values):
    sigma = jax.nn.sigmoid(values)
    return sigma * (1.0 + values * (1.0 - sigma))


def advance_layer(packed):
    inputs, weight, layer_gain = packed
    pre_act = jnp.dot(inputs, weight, preferred_element_type=jnp.float32)
    return (inputs.astype(jnp.float32) + layer_gain * jax.nn.silu(pre_act)).astype(jnp.bfloat16)


def retreat_layer(packed):
    upstream, stored, weight, layer_gain = packed
    pre_act = jnp.dot(stored, weight, preferred_element_type=jnp.float32)
    scaled = (upstream.astype(jnp.float32) * layer_gain * silu_slope(pre_act)).astype(jnp.bfloat16)
    back_term = jnp.dot(scaled, weight.T, preferred_element_type=jnp.float32)
    return (upstream.astype(jnp.float32) + back_term).astype(jnp.bfloat16)


def reference(weights, layer_gains, incoming, fresh_batch, returning, fresh_cotangent, stashed_inputs):
    first_out = lax.map(advance_layer, (incoming, weights, layer_gains))
    feed = jnp.concatenate([fresh_batch[None], first_out[:-1]], axis=0)
    second_out = lax.map(advance_layer, (feed, weights, layer_gains))
    grad_first = lax.map(retreat_layer, (returning, stashed_inputs[:, 0], weights, layer_gains))
    upstream = jnp.concatenate([grad_first[1:], fresh_cotangent[None]], axis=0)
    grad_second = lax.map(retreat_layer, (upstream, stashed_inputs[:, 1], weights, layer_gains))
    layer_outputs = jnp.stack([first_out, second_out], axis=1)
    input_grads = jnp.stack([grad_first, grad_second], axis=1)
    return layer_outputs, input_grads
```

```python
import jax
import jax.numpy as jnp
from jax import lax
from jax.sharding import PartitionSpec as P

F32 = jnp.float32
BF16 = jnp.bfloat16


def silu_slope(values):
    sigma = jax.nn.sigmoid(values)
    return sigma * (1.0 + values * (1.0 - sigma))


def passed_along(value, steps):
    count = lax.axis_size("segment")
    first, last = (max(0, -steps), min(count, count - steps))
    return lax.ppermute(value, "segment", [(source, source + steps) for source in range(first, last)])


def rows_swapped(value, flip):
    count = lax.axis_size("row")
    return lax.ppermute(value, "row", [(source, source ^ flip) for source in range(count)])


def plane_sent(value, pairs):
    cols = lax.axis_size("col")
    return lax.ppermute(
        value, ("row", "col"), [(a * cols + b, c * cols + d) for (a, b), (c, d) in pairs]
    )


def bits_of(count):
    return count.bit_length() - 1


def pick(blocks, which):
    chosen = blocks[0]
    for at in range(1, len(blocks)):
        chosen = jnp.where(which == at, blocks[at], chosen)
    return chosen


class Plane:
    def __init__(self, weight_block):
        self.rows, self.cols = lax.axis_size("row"), lax.axis_size("col")
        self.per_col = self.rows // self.cols
        self.row, self.col = lax.axis_index("row"), lax.axis_index("col")
        self.steps = bits_of(self.rows)
        self.streams = max(self.steps, 1)
        self.home = self.row // self.per_col
        self.at_home = self.col == self.home
        self.within = self.row % self.per_col
        width = weight_block.shape[1] // self.streams
        self.weight_parts = [
            weight_block[:, at * width : (at + 1) * width] for at in range(self.streams)
        ]

    def features_in(self, block):
        width = block.shape[1] // self.per_col
        pieces = [block[:, at * width : (at + 1) * width] for at in range(self.per_col)]
        relative = [
            pick([pieces[at ^ shift] for at in range(self.per_col)], self.within)
            for shift in range(self.per_col)
        ]
        gathered = [relative[0]]
        for flip in range(1, self.rows):
            pairs = [
                ((r, (r ^ flip) // self.per_col), (r ^ flip, (r ^ flip) // self.per_col))
                for r in range(self.rows)
            ]
            gathered.append(plane_sent(relative[flip % self.per_col], pairs))
        whole = jnp.concatenate(gathered, axis=0)
        shared = whole
        for shift in range(1, self.cols):
            pairs = [
                ((r, r // self.per_col), (r, (r // self.per_col) ^ shift)) for r in range(self.rows)
            ]
            shared = jnp.where(
                (self.col ^ self.home) == shift, plane_sent(whole, pairs), shared
            )
        return shared

    def features_out(self, partial):
        total = partial.astype(F32)
        sent = partial.astype(BF16)
        for shift in range(1, self.cols):
            pairs = [
                ((r, (r // self.per_col) ^ shift), (r, r // self.per_col)) for r in range(self.rows)
            ]
            total = total + plane_sent(sent, pairs).astype(F32)
        total = total.astype(BF16)
        tokens = total.shape[0] // self.rows
        arrived = [total[:tokens]]
        for flip in range(1, self.rows):
            pairs = [((r, r // self.per_col), (r ^ flip, r // self.per_col)) for r in range(self.rows)]
            arrived.append(plane_sent(total[flip * tokens : (flip + 1) * tokens], pairs))
        relative = []
        for shift in range(self.per_col):
            found = arrived[shift]
            for group in range(1, self.cols):
                found = jnp.where(
                    (self.col ^ self.home) == group, arrived[group * self.per_col + shift], found
                )
            relative.append(found)
        return jnp.concatenate(
            [
                pick([relative[at ^ within] for within in range(self.per_col)], self.within)
                for at in range(self.per_col)
            ],
            axis=1,
        )

    def forward(self, full):
        tokens = full.shape[0] // self.rows
        summed = []
        for stream, weight in enumerate(self.weight_parts):
            product = jnp.dot(full, weight, preferred_element_type=F32).astype(BF16)
            held = {k: product[k * tokens : (k + 1) * tokens] for k in range(self.rows)}
            summed.append(held)
        for step in range(self.steps):
            for stream in range(self.streams):
                held = summed[stream]
                flip = 1 << ((stream + step) % self.steps)
                away = [k for k in sorted(held) if k & flip]
                arrived = rows_swapped(
                    jnp.concatenate([held[k].astype(BF16) for k in away], axis=0), flip
                )
                summed[stream] = {
                    k ^ flip: held[k ^ flip].astype(F32)
                    + arrived[at * tokens : (at + 1) * tokens].astype(F32)
                    for at, k in enumerate(away)
                }
        return jnp.concatenate([held[0].astype(F32) for held in summed], axis=1)

    def backward(self, scaled):
        width = scaled.shape[1] // self.streams
        pieces = [
            {0: scaled[:, at * width : (at + 1) * width]} for at in range(self.streams)
        ]
        for step in range(self.steps):
            for stream in range(self.streams):
                held = pieces[stream]
                tokens = scaled.shape[0]
                flip = 1 << ((stream + step) % self.steps)
                ours = sorted(held)
                arrived = rows_swapped(jnp.concatenate([held[k] for k in ours], axis=0), flip)
                for at, k in enumerate(ours):
                    held[k ^ flip] = arrived[at * tokens : (at + 1) * tokens]
        partial = 0.0
        for held, weight in zip(pieces, self.weight_parts):
            whole = jnp.concatenate([held[k] for k in range(self.rows)], axis=0)
            partial = partial + lax.dot_general(
                whole, weight, (((1,), (1,)), ((), ())), preferred_element_type=F32
            )
        return partial


def shards(weights, layer_gains, incoming, fresh_batch, returning, fresh_cotangent, stashed_inputs):
    segment_index = lax.axis_index("segment")
    segment_count = lax.axis_size("segment")
    plane = Plane(weights[0])
    layer_gain = layer_gains[0][None, :]

    def advance(own_block, full_input):
        pre_act = plane.forward(full_input)
        return (own_block.astype(F32) + layer_gain * jax.nn.silu(pre_act)).astype(BF16)

    def retreat(upstream, pre_act):
        scaled = (upstream.astype(F32) * layer_gain * silu_slope(pre_act)).astype(BF16)
        back_term = plane.features_out(plane.backward(scaled)).astype(F32)
        return (upstream.astype(F32) + back_term).astype(BF16)

    first_stored = plane.features_in(stashed_inputs[0, 0])
    full_input = plane.features_in(incoming[0])
    second_stored = plane.features_in(stashed_inputs[0, 1])

    first_back_pre = plane.forward(first_stored)
    grad_first = retreat(returning[0], first_back_pre)
    first_out = advance(incoming[0], full_input)
    second_back_pre = plane.forward(second_stored)

    arrived = passed_along(first_out, 1)
    feed_block = jnp.where(segment_index == 0, fresh_batch, arrived)
    arrived_grad = passed_along(grad_first, -1)
    upstream = jnp.where(segment_index == segment_count - 1, fresh_cotangent, arrived_grad)
    second_out = advance(feed_block, plane.features_in(feed_block))
    grad_second = retreat(upstream, second_back_pre)
    layer_outputs = jnp.stack([first_out, second_out], axis=0)[None]
    input_grads = jnp.stack([grad_first, grad_second], axis=0)[None]
    return (layer_outputs, input_grads)


def solution(mesh):
    in_specs = (
        P("segment", "row", "col"),
        P("segment", "col"),
        P("segment", "row", "col"),
        P("row", "col"),
        P("segment", "row", "col"),
        P("row", "col"),
        P("segment", None, "row", "col"),
    )
    out_specs = (P("segment", None, "row", "col"), P("segment", None, "row", "col"))
    return jax.shard_map(shards, mesh=mesh, in_specs=in_specs, out_specs=out_specs, check_vma=False)
```

```python
import jax
import jax.numpy as jnp
from jax import lax
from jax.sharding import PartitionSpec as P

F32 = jnp.float32
BF16 = jnp.bfloat16


def silu_slope(values):
    sigma = jax.nn.sigmoid(values)
    return sigma * (1.0 + values * (1.0 - sigma))


def passed_along(value, steps):
    count = lax.axis_size("segment")
    first, last = (max(0, -steps), min(count, count - steps))
    return lax.ppermute(value, "segment", [(source, source + steps) for source in range(first, last)])


def after(value, other):
    return lax.optimization_barrier((value, other))[0]


def bits_of(count):
    return count.bit_length() - 1


def xor_order(blocks, index):
    for bit in range(bits_of(len(blocks))):
        flip = 1 << bit
        is_set = (index & flip) != 0
        blocks = [
            jnp.where(is_set, blocks[k ^ flip], blocks[k]) for k in range(len(blocks))
        ]
    return blocks


def cut(value, count, axis=0):
    return jnp.split(value, count, axis=axis)


def row_swap(value, flip):
    count = lax.axis_size("row")
    return lax.ppermute(value, "row", [(source, source ^ flip) for source in range(count)])


def col_swap(value, flip):
    count = lax.axis_size("col")
    return lax.ppermute(value, "col", [(source, source ^ flip) for source in range(count)])


class Plane:
    def __init__(self, weight):
        self.weight = weight
        self.rows, self.cols = lax.axis_size("row"), lax.axis_size("col")
        self.row, self.col = lax.axis_index("row"), lax.axis_index("col")
        self.steps = bits_of(self.rows)

    def flips(self, col):
        return [1 << ((col + step) % self.steps) for step in range(self.steps)]

    def places(self, col):
        flips = self.flips(col)
        return [
            sum(flip for at, flip in enumerate(flips) if place >> (self.steps - 1 - at) & 1)
            for place in range(self.rows)
        ]

    def by_place(self, blocks):
        orders = [[blocks[k] for k in self.places(col)] for col in range(max(self.steps, 1))]
        return self.choose(orders)

    def by_k(self, blocks):
        orders = []
        for col in range(max(self.steps, 1)):
            places = self.places(col)
            orders.append([blocks[places.index(k)] for k in range(self.rows)])
        return self.choose(orders)

    def choose(self, orders):
        chosen = orders[0]
        for at in range(1, len(orders)):
            picked = self.col % len(orders) == at
            chosen = [
                old if old is new else jnp.where(picked, new, old)
                for old, new in zip(chosen, orders[at])
            ]
        return chosen

    def step_swap(self, value, step):
        pairs = []
        for row in range(self.rows):
            for col in range(self.cols):
                other = row ^ self.flips(col)[step]
                pairs.append((row * self.cols + col, other * self.cols + col))
        return lax.ppermute(value, ("row", "col"), pairs)

    def exchanged(self, value):
        return [value] + [col_swap(value, flip) for flip in range(1, self.cols)]

    def wanted(self, columns):
        mine = xor_order(cut(columns, self.cols), self.col)[0]
        return xor_order(cut(mine, self.rows, axis=1), self.row)

    def sent(self, blocks):
        return blocks[:1] + [row_swap(blocks[k], k) for k in range(1, self.rows)]

    def spread(self, block):
        parts = xor_order(cut(block, self.cols), self.col)
        pieces = [parts[0]] + [col_swap(parts[flip], flip) for flip in range(1, self.cols)]
        columns = jnp.concatenate(xor_order(pieces, self.col), axis=1)
        return self.sent(xor_order(cut(columns, self.rows, axis=1), self.row))

    def joined(self, arrived):
        half = jnp.concatenate(arrived, axis=0)
        halves = [half] + [col_swap(half, flip) for flip in range(1, self.cols)]
        ordered = [cut(h, self.rows) for h in xor_order(halves, self.col)]
        return [jnp.concatenate([h[k] for h in ordered], axis=0) for k in range(self.rows)]

    def product(self, blocks):
        full = jnp.concatenate(self.by_place(blocks), axis=0)
        return jnp.dot(full, self.weight, preferred_element_type=F32).astype(BF16)

    def summed(self, partial, waits=()):
        total, messages = partial, []
        for step in range(self.steps):
            ours, away = cut(total, 2)
            messages.append(away.astype(BF16))
            arrived = self.step_swap(messages[-1], step)
            if step < len(waits):
                arrived = after(arrived, waits[step])
            total = ours.astype(F32) + arrived.astype(F32)
        return total.astype(F32), messages

    def gathered(self, block):
        messages = []
        for step in reversed(range(self.steps)):
            messages.append(block)
            block = jnp.concatenate([block, self.step_swap(block, step)], axis=0)
        return block, messages

    def returned(self, scaled):
        partial = lax.dot_general(
            scaled, self.weight, (((1,), (1,)), ((), ())), preferred_element_type=F32
        ).astype(BF16)
        blocks = [cut(block, self.cols) for block in self.by_k(cut(partial, self.rows))]
        shares = xor_order(
            [jnp.concatenate([b[at] for b in blocks], axis=0) for at in range(self.cols)], self.col
        )
        total = shares[0].astype(F32)
        for flip in range(1, self.cols):
            total = total + col_swap(shares[flip], flip).astype(F32)
        total = total.astype(BF16)
        arrived = self.sent(cut(total, self.rows))
        columns = jnp.concatenate(xor_order(arrived, self.row), axis=1)
        pieces = xor_order(cut(columns, self.cols, axis=1), self.col)
        last = pieces[0]
        pieces = pieces[:1] + [col_swap(pieces[flip], flip) for flip in range(1, self.cols)]
        return jnp.concatenate(xor_order(pieces, self.col), axis=0), [shares[0], total, last]


def shards(weights, layer_gains, incoming, fresh_batch, returning, fresh_cotangent, stashed_inputs):
    segment_index = lax.axis_index("segment")
    segment_count = lax.axis_size("segment")
    plane = Plane(weights[0])
    layer_gain = layer_gains[0][None, :]

    def advance(own_block, pre_act):
        return (own_block.astype(F32) + layer_gain * jax.nn.silu(pre_act)).astype(BF16)

    def scale(upstream, pre_act):
        return (upstream.astype(F32) * layer_gain * silu_slope(pre_act)).astype(BF16)

    def retreat(upstream, back_term):
        return (upstream.astype(F32) + back_term.astype(F32)).astype(BF16)

    def side_by_side(pieces):
        return jnp.concatenate(xor_order(pieces, plane.col), axis=-1)

    stored = side_by_side(plane.exchanged(stashed_inputs[0]))
    entering = side_by_side(plane.exchanged(incoming[0]))
    batches = [stored[0], entering, stored[1]]
    spread = plane.sent(
        [jnp.concatenate(blocks, axis=0) for blocks in zip(*map(plane.wanted, batches))]
    )
    spread = [cut(block, len(batches)) for block in spread]
    first_spread = [block[0] for block in spread]
    rest_spread = [jnp.concatenate(block[1:], axis=0) for block in spread]

    first_back = plane.product(plane.joined(first_spread))
    back_pre, back_sent = plane.summed(first_back)
    scaled_first = scale(returning[0], back_pre)
    gathered_first, gather_sent = plane.gathered(scaled_first)
    back_first, return_sent = plane.returned(gathered_first)
    grad_first = retreat(returning[0], back_first)

    rest = plane.joined([after(block, back_sent[0]) for block in rest_spread])
    rest = [cut(block, 2 * plane.cols) for block in rest]
    entered = [jnp.concatenate(block[0::2], axis=0) for block in rest]
    second_stored = [jnp.concatenate(block[1::2], axis=0) for block in rest]
    first_pre, _ = plane.summed(plane.product(entered), [gather_sent[0], gather_sent[1]])
    first_out = advance(incoming[0], first_pre)
    arrived = passed_along(first_out, 1)
    second_back_pre, _ = plane.summed(
        plane.product([after(block, first_out) for block in second_stored]),
        [return_sent[1], grad_first],
    )
    feed_block = jnp.where(segment_index == 0, fresh_batch, after(arrived, return_sent[0]))
    feed_spread = [after(block, grad_first) for block in plane.spread(feed_block)]
    second_partial = plane.product(plane.joined(feed_spread))

    arrived_grad = after(passed_along(grad_first, -1), first_out)
    upstream = jnp.where(segment_index == segment_count - 1, fresh_cotangent, arrived_grad)
    scaled_second = scale(upstream, second_back_pre)
    gathered_second, gather_sent = plane.gathered(scaled_second)
    back_second, return_sent = plane.returned(gathered_second)
    grad_second = retreat(upstream, back_second)
    second_pre, _ = plane.summed(second_partial, [gather_sent[0], return_sent[0]])
    second_out = advance(feed_block, second_pre)
    layer_outputs = jnp.stack([first_out, second_out], axis=0)[None]
    input_grads = jnp.stack([grad_first, grad_second], axis=0)[None]
    return (layer_outputs, input_grads)


def solution(mesh):
    in_specs = (
        P("segment", "row", "col"),
        P("segment", "col"),
        P("segment", "row", "col"),
        P("row", "col"),
        P("segment", "row", "col"),
        P("row", "col"),
        P("segment", None, "row", "col"),
    )
    out_specs = (P("segment", None, "row", "col"), P("segment", None, "row", "col"))
    return jax.shard_map(shards, mesh=mesh, in_specs=in_specs, out_specs=out_specs, check_vma=False)
```

```python
import jax
import jax.numpy as jnp
from jax import lax
from jax.sharding import PartitionSpec as P

F32 = jnp.float32
BF16 = jnp.bfloat16


def silu_slope(values):
    sigma = jax.nn.sigmoid(values)
    return sigma * (1.0 + values * (1.0 - sigma))


def passed_along(value, steps):
    count = lax.axis_size("segment")
    first, last = (max(0, -steps), min(count, count - steps))
    return lax.ppermute(value, "segment", [(source, source + steps) for source in range(first, last)])


def after(value, other):
    return value if other is None else lax.optimization_barrier((value, other))[0]


def bits_of(count):
    return count.bit_length() - 1


def xor_order(blocks, index):
    for bit in range(bits_of(len(blocks))):
        flip = 1 << bit
        is_set = (index & flip) != 0
        blocks = [
            jnp.where(is_set, blocks[k ^ flip], blocks[k]) for k in range(len(blocks))
        ]
    return blocks


def cut(value, count, axis=0):
    return jnp.split(value, count, axis=axis)


def row_swap(value, flip):
    count = lax.axis_size("row")
    return lax.ppermute(value, "row", [(source, source ^ flip) for source in range(count)])


def col_swap(value, flip):
    count = lax.axis_size("col")
    return lax.ppermute(value, "col", [(source, source ^ flip) for source in range(count)])


class Plane:
    def __init__(self, weight):
        self.weight = weight
        self.rows, self.cols = lax.axis_size("row"), lax.axis_size("col")
        self.row, self.col = lax.axis_index("row"), lax.axis_index("col")
        self.steps = bits_of(self.rows)
        self.per_col = self.rows // self.cols

    def flips(self, col):
        return [1 << ((col + step) % self.steps) for step in range(self.steps)]

    def places(self, col):
        flips = self.flips(col)
        return [
            sum(flip for at, flip in enumerate(flips) if place >> (self.steps - 1 - at) & 1)
            for place in range(self.rows)
        ]

    def by_place(self, blocks):
        orders = [[blocks[k] for k in self.places(col)] for col in range(max(self.steps, 1))]
        return self.choose(orders)

    def by_k(self, blocks):
        orders = []
        for col in range(max(self.steps, 1)):
            places = self.places(col)
            orders.append([blocks[places.index(k)] for k in range(self.rows)])
        return self.choose(orders)

    def choose(self, orders):
        chosen = orders[0]
        for at in range(1, len(orders)):
            picked = self.col % len(orders) == at
            chosen = [
                old if old is new else jnp.where(picked, new, old)
                for old, new in zip(chosen, orders[at])
            ]
        return chosen

    def step_swap(self, value, step):
        pairs = []
        for row in range(self.rows):
            for col in range(self.cols):
                other = row ^ self.flips(col)[step]
                pairs.append((row * self.cols + col, other * self.cols + col))
        return lax.ppermute(value, ("row", "col"), pairs)

    def home_of(self, row):
        return row // self.per_col

    def across(self, value, shift, onward=0):
        pairs = []
        for row in range(self.rows):
            home = self.home_of(row)
            for j in range(self.cols):
                other = row ^ (j * self.per_col + shift)
                pairs.append((row * self.cols + (home ^ j), other * self.cols + home))
        if not onward:
            return lax.ppermute(value, ("row", "col"), pairs)
        sections, size = lax.axis_size("segment"), self.rows * self.cols
        pairs = [
            (at * size + source, (at + onward) * size + target)
            for at in range(sections)
            if 0 <= at + onward < sections
            for source, target in pairs
        ]
        return lax.ppermute(value, ("segment", "row", "col"), pairs)

    def spread(self, block):
        pieces = xor_order(cut(block, self.per_col, axis=1), self.row % self.per_col)
        return [self.across(piece, shift) for shift, piece in enumerate(pieces)]

    def joined(self, arrived):
        half = jnp.concatenate(arrived, axis=0)
        halves = [half] + [col_swap(half, flip) for flip in range(1, self.cols)]
        halves = xor_order(halves, self.col ^ self.home_of(self.row))
        return [block for half in halves for block in cut(half, self.per_col)]

    def product(self, blocks):
        full = jnp.concatenate(self.by_place(blocks), axis=0)
        return jnp.dot(full, self.weight, preferred_element_type=F32).astype(BF16)

    def halved(self, total, step, wait=None):
        if step >= self.steps:
            return total, None
        ours, away = cut(total, 2)
        message = lax.optimization_barrier(away.astype(BF16))
        arrived = after(self.step_swap(message, step), wait)
        return ours.astype(F32) + arrived.astype(F32), message

    def doubled(self, block, step, wait=None):
        if step >= self.steps:
            return block, None
        block = lax.optimization_barrier(block)
        arrived = after(self.step_swap(block, step), wait)
        return jnp.concatenate([block, arrived], axis=0), block

    def transposed(self, scaled):
        return lax.dot_general(
            scaled, self.weight, (((1,), (1,)), ((), ())), preferred_element_type=F32
        ).astype(BF16)

    def shares(self, partial):
        ordered = jnp.concatenate(self.by_k(cut(partial, self.rows)), axis=0)
        shares = xor_order(cut(ordered, self.cols), self.col ^ self.home_of(self.row))
        return lax.optimization_barrier(shares)

    def shared(self, shares, wait=None):
        total = shares[0].astype(F32)
        for flip in range(1, self.cols):
            total = total + after(col_swap(shares[flip], flip), wait).astype(F32)
        return lax.optimization_barrier(total.astype(BF16))

    def delivered(self, total, onward=0):
        pieces = cut(total, self.per_col)
        arrived = [self.across(piece, at, onward) for at, piece in enumerate(pieces)]
        return jnp.concatenate(xor_order(arrived, self.row % self.per_col), axis=1)


def shards(weights, layer_gains, incoming, fresh_batch, returning, fresh_cotangent, stashed_inputs):
    segment_index = lax.axis_index("segment")
    segment_count = lax.axis_size("segment")
    plane = Plane(weights[0])
    layer_gain = layer_gains[0][None, :]

    def advance(own_block, pre_act):
        return (own_block.astype(F32) + layer_gain * jax.nn.silu(pre_act)).astype(BF16)

    def scale(upstream, pre_act):
        return (upstream.astype(F32) * layer_gain * silu_slope(pre_act)).astype(BF16)

    def retreat(upstream, back_term):
        return (upstream.astype(F32) + back_term.astype(F32)).astype(BF16)

    tokens, steps = incoming.shape[1], plane.steps
    spread = plane.spread(jnp.concatenate([stashed_inputs[0, 0], incoming[0], stashed_inputs[0, 1]]))
    first_stored = plane.joined([block[:tokens] for block in spread])
    rest = plane.joined([block[tokens:] for block in spread])
    entered = [block[:tokens] for block in rest]
    second_stored = [block[tokens:] for block in rest]
    returning_ahead = passed_along(returning[0], -1)

    first_back = after(plane.product(first_stored), rest[0])
    first_pre = plane.product([after(block, first_back) for block in entered])
    first_back, _ = plane.halved(first_back, 0, first_pre)
    first_back = lax.optimization_barrier(first_back)
    first_pre, _ = plane.halved(first_pre, 0, first_back)
    for step in range(1, steps):
        first_back, _ = plane.halved(first_back, step, first_pre)
    scaled_first = lax.optimization_barrier(scale(returning[0], first_back))
    for step in range(1, steps):
        first_pre, _ = plane.halved(first_pre, step, scaled_first)
    first_out = lax.optimization_barrier(advance(incoming[0], first_pre))
    arrived = passed_along(first_out, 1)

    second_back = plane.product([after(block, first_out) for block in second_stored])
    gathered = scaled_first
    for step in reversed(range(1, steps)):
        gathered, _ = plane.doubled(gathered, step, first_out)
    gathered, _ = plane.doubled(gathered, 0, second_back)
    partial = plane.transposed(gathered)
    feed_block = jnp.where(segment_index == 0, fresh_batch, after(arrived, partial))
    shares = plane.shares(after(partial, feed_block))
    second_back, _ = plane.halved(second_back, 0, shares[-1])
    total = plane.shared(shares)
    feed_spread = plane.spread(after(feed_block, total))
    for step in range(1, steps):
        second_back, _ = plane.halved(second_back, step, total)
    arrived_grad = retreat(after(returning_ahead, total), plane.delivered(total, -1))
    grad_first = retreat(returning[0], plane.delivered(total))

    upstream = jnp.where(segment_index == segment_count - 1, fresh_cotangent, arrived_grad)
    scaled_second = lax.optimization_barrier(scale(upstream, second_back))
    second_pre = plane.product(plane.joined([after(block, scaled_second) for block in feed_spread]))
    gathered = scaled_second
    for step in reversed(range(1, steps)):
        gathered, _ = plane.doubled(gathered, step, second_pre)
    gathered = lax.optimization_barrier(gathered)
    second_pre, _ = plane.halved(second_pre, 0, gathered)
    gathered, _ = plane.doubled(gathered, 0, second_pre)
    shares = plane.shares(plane.transposed(gathered))
    grad_first = after(grad_first, shares[-1])
    total = plane.shared(shares)
    for step in range(1, steps):
        second_pre, _ = plane.halved(second_pre, step, total)
    second_out = advance(feed_block, second_pre)
    grad_second = retreat(upstream, plane.delivered(total))
    layer_outputs = jnp.stack([first_out, second_out], axis=0)[None]
    input_grads = jnp.stack([grad_first, grad_second], axis=0)[None]
    return (layer_outputs, input_grads)


def solution(mesh):
    in_specs = (
        P("segment", "row", "col"),
        P("segment", "col"),
        P("segment", "row", "col"),
        P("row", "col"),
        P("segment", "row", "col"),
        P("row", "col"),
        P("segment", None, "row", "col"),
    )
    out_specs = (P("segment", None, "row", "col"), P("segment", None, "row", "col"))
    return jax.shard_map(shards, mesh=mesh, in_specs=in_specs, out_specs=out_specs, check_vma=False)
```

```python
import jax
import jax.numpy as jnp
from jax import lax
from jax.sharding import PartitionSpec as P

F32 = jnp.float32
BF16 = jnp.bfloat16

TURNED = ("B0", "G1")
AT_ONCE = ("A0", "A1", "G0")
GATES = {
    "A0_o": ("weight",),
    "A1_a0": ("A0_x",),
    "A1_in": ("A0_m0",),
    "A1_s": ("B0_m0",),
    "A2_a0": ("B0_m1",),
    "A2_in": ("B0_m0",),
    "A2_o": ("A2_a0",),
    "A2_s": ("B0_m1",),
    "A3_a0": ("A3_m1",),
    "A3_a1": ("sc2",),
    "A3_in": ("zf_a",),
    "B0_a0": ("F1_t0",),
    "B0_a1": ("F1_m1",),
    "B1_a0": ("G0_h",),
    "B1_a1": ("G0_s",),
    "B1_x": ("out1",),
    "D0_a0": ("feed",),
    "F1_a1": ("sc1",),
    "F2_a0": ("G1_m1",),
    "F2_a1": ("G1_s",),
    "F2_x": ("A3_o",),
    "G0_a0": ("out1",),
    "G0_a1": ("B1_t0",),
    "G0_h": ("B1_t0", "feed"),
    "G1_a0": ("F2_t0",),
    "G1_a1": ("F2_m1",),
    "G1_h": ("G1_m1",),
    "W0_m": ("G0_m1",),
    "gr1": ("F2_t0",),
    "out2": ("G1_m1",),
    "zr_m": ("B0_m1",),
}


def silu_slope(values):
    sigma = jax.nn.sigmoid(values)
    return sigma * (1.0 + values * (1.0 - sigma))


def passed_along(value, steps):
    count = lax.axis_size("segment")
    first, last = (max(0, -steps), min(count, count - steps))
    return lax.ppermute(value, "segment", [(source, source + steps) for source in range(first, last)])


def fixed(value):
    return lax.optimization_barrier(value)


def bits_of(count):
    return count.bit_length() - 1


def cut(value, count, axis=0):
    return jnp.split(value, count, axis=axis)


def xor_order(blocks, index):
    for bit in range(bits_of(len(blocks))):
        flip = 1 << bit
        is_set = (index & flip) != 0
        blocks = [jnp.where(is_set, blocks[k ^ flip], blocks[k]) for k in range(len(blocks))]
    return blocks


def col_swap(value, flip):
    count = lax.axis_size("col")
    return lax.ppermute(value, "col", [(source, source ^ flip) for source in range(count)])


class Plane:
    def __init__(self):
        self.rows, self.cols = lax.axis_size("row"), lax.axis_size("col")
        self.row, self.col = lax.axis_index("row"), lax.axis_index("col")
        self.steps = bits_of(self.rows)
        self.per_col = self.rows // self.cols
        self.home = self.row // self.per_col

    def flips(self, col, turn):
        return [1 << ((col + turn + step) % self.steps) for step in range(self.steps)]

    def places(self, col, turn):
        flips = self.flips(col, turn)
        return [
            sum(flip for at, flip in enumerate(flips) if place >> (self.steps - 1 - at) & 1)
            for place in range(self.rows)
        ]

    def choose(self, orders):
        chosen = orders[0]
        for at in range(1, len(orders)):
            picked = self.col % len(orders) == at
            chosen = [
                old if old is new else jnp.where(picked, new, old)
                for old, new in zip(chosen, orders[at])
            ]
        return chosen

    def by_place(self, blocks, turn):
        kinds = range(max(self.steps, 1))
        return self.choose([[blocks[k] for k in self.places(col, turn)] for col in kinds])

    def by_k(self, blocks, turn):
        orders = []
        for col in range(max(self.steps, 1)):
            places = self.places(col, turn)
            orders.append([blocks[places.index(k)] for k in range(self.rows)])
        return self.choose(orders)

    def step_swap(self, value, step, turn):
        pairs = []
        for row in range(self.rows):
            for col in range(self.cols):
                other = row ^ self.flips(col, turn)[step]
                pairs.append((row * self.cols + col, other * self.cols + col))
        return lax.ppermute(value, ("row", "col"), pairs)

    def across(self, value, shift, onward=0):
        pairs = []
        for row in range(self.rows):
            home = row // self.per_col
            for j in range(self.cols):
                other = row ^ (j * self.per_col + shift)
                pairs.append((row * self.cols + (home ^ j), other * self.cols + home))
        if not onward:
            return lax.ppermute(value, ("row", "col"), pairs)
        sections, size = lax.axis_size("segment"), self.rows * self.cols
        pairs = [
            (at * size + source, (at + onward) * size + target)
            for at in range(sections)
            if 0 <= at + onward < sections
            for source, target in pairs
        ]
        return lax.ppermute(value, ("segment", "row", "col"), pairs)

    def joined(self, half, others, at_once):
        if at_once:
            halves = xor_order(others, self.home)
        else:
            halves = xor_order([half] + others, self.col ^ self.home)
        return [block for half in halves for block in cut(half, self.per_col)]

    def shares(self, partial, turn):
        ordered = jnp.concatenate(self.by_k(cut(partial, self.rows), turn), axis=0)
        return xor_order(cut(ordered, self.cols), self.col ^ self.home)

    def in_columns(self, arrived):
        return jnp.concatenate(xor_order(arrived, self.row % self.per_col), axis=1)


class Flow:
    def __init__(self, gates):
        self.gates, self.rules, self.values = gates, {}, {}

    def rule(self, name, make):
        self.rules[name] = make

    def __call__(self, name):
        if name not in self.values:
            value = self.rules[name]()
            others = [self(other) for other in self.gates.get(name, ()) if other in self.rules]
            if others:
                value = lax.optimization_barrier((value, others))[0]
            self.values[name] = value
        return self.values[name]


def shards(weights, layer_gains, incoming, fresh_batch, returning, fresh_cotangent, stashed_inputs):
    segment_index = lax.axis_index("segment")
    segment_count = lax.axis_size("segment")
    layer_gain = layer_gains[0][None, :]
    plane = Plane()
    steps, shifts = plane.steps, range(plane.per_col)
    flow = Flow(GATES)
    rule = flow.rule

    def advance(own_block, pre_act):
        return fixed((own_block.astype(F32) + layer_gain * jax.nn.silu(pre_act)).astype(BF16))

    def scale(upstream, pre_act):
        return fixed((upstream.astype(F32) * layer_gain * silu_slope(pre_act)).astype(BF16))

    def retreat(upstream, back_term):
        return (upstream.astype(F32) + back_term.astype(F32)).astype(BF16)

    def spread(name, block):
        def message(shift):
            pieces = cut(flow(f"{name}_in"), plane.per_col, axis=1)
            return xor_order(pieces, plane.row % plane.per_col)[shift]

        def others():
            half = flow(f"{name}_s")
            if name in AT_ONCE:
                halves = lax.all_gather(half, "col", axis=0, tiled=False)
                return [halves[col] for col in range(plane.cols)]
            return [col_swap(half, flip) for flip in range(1, plane.cols)]

        rule(f"{name}_in", block)
        for shift in shifts:
            rule(f"{name}_m{shift}", lambda shift=shift: message(shift))
            rule(f"{name}_a{shift}", lambda shift=shift: plane.across(flow(f"{name}_m{shift}"), shift))
        rule(f"{name}_s", lambda: jnp.concatenate([flow(f"{name}_a{at}") for at in shifts], axis=0))
        rule(f"{name}_o", others)
        rule(f"{name}_x", lambda: plane.joined(flow(f"{name}_s"), flow(f"{name}_o"), name in AT_ONCE))

    def product(name, source):
        turn = int(name in TURNED)

        def multiplied():
            full = jnp.concatenate(plane.by_place(flow(f"{name}_x"), turn), axis=0)
            return jnp.dot(full, flow("weight"), preferred_element_type=F32).astype(BF16)

        def message(step):
            return fixed(cut(flow(f"{name}_t{step}"), 2)[1].astype(BF16))

        def total(step):
            ours = cut(flow(f"{name}_t{step}"), 2)[0]
            return ours.astype(F32) + flow(f"{name}_a{step}").astype(F32)

        rule(f"{name}_x", lambda: flow(f"{source}_x"))
        rule(f"{name}_t0", multiplied)
        for step in range(steps):
            rule(f"{name}_m{step}", lambda step=step: message(step))
            rule(
                f"{name}_a{step}",
                lambda step=step: plane.step_swap(flow(f"{name}_m{step}"), step, turn),
            )
            rule(f"{name}_t{step + 1}", lambda step=step: total(step))
        return lambda: flow(f"{name}_t{steps}").astype(F32)

    def back(name, scaled):
        turn = int(name in TURNED)

        def doubled(at):
            block = jnp.concatenate([flow(f"{name}_m{at}"), flow(f"{name}_a{at}")], axis=0)
            return fixed(block) if at + 1 < steps else block

        def multiplied():
            return lax.dot_general(
                flow(f"{name}_m{steps}"),
                flow("weight"),
                (((1,), (1,)), ((), ())),
                preferred_element_type=F32,
            ).astype(BF16)

        def others():
            shares = flow(f"{name}_h")
            if name in AT_ONCE and plane.cols == 2:
                both = lax.all_gather(shares[1], "col", axis=0, tiled=False)
                return [jnp.where(plane.col == 0, both[1], both[0])]
            return [col_swap(shares[flip], flip) for flip in range(1, plane.cols)]

        def total():
            ours = flow(f"{name}_h")[0].astype(F32)
            return fixed(sum([o.astype(F32) for o in flow(f"{name}_o")], ours).astype(BF16))

        rule(f"{name}_m0", lambda: flow(scaled))
        for at in range(steps):
            step = steps - 1 - at
            rule(
                f"{name}_a{at}",
                lambda at=at, step=step: plane.step_swap(flow(f"{name}_m{at}"), step, turn),
            )
            rule(f"{name}_m{at + 1}", lambda at=at: doubled(at))
        rule(f"{name}_p", multiplied)
        rule(f"{name}_h", lambda: fixed(plane.shares(flow(f"{name}_p"), turn)))
        rule(f"{name}_o", others)
        rule(f"{name}_s", total)

    def deliver(name, source, onward=0):
        rule(f"{name}_m", lambda: cut(flow(source), plane.per_col))
        for shift in shifts:
            rule(
                f"{name}_a{shift}",
                lambda shift=shift: plane.across(flow(f"{name}_m")[shift], shift, onward),
            )
        return lambda: plane.in_columns([flow(f"{name}_a{shift}") for shift in shifts])

    rule("weight", lambda: weights[0])

    spread("A0", lambda: stashed_inputs[0, 0])
    spread("A1", lambda: incoming[0])
    spread("A2", lambda: stashed_inputs[0, 1])
    first_back, first_pre, second_back = product("B0", "A0"), product("F1", "A1"), product("B1", "A2")
    rule("sc1", lambda: scale(returning[0], first_back()))
    rule("out1", lambda: advance(incoming[0], first_pre()))
    back("G0", "sc1")
    own_back = deliver("W0", "G0_s")
    rule("gr1", lambda: retreat(returning[0], own_back()))

    rule("zf_a", lambda: passed_along(flow("out1"), 1))
    rule("feed", lambda: jnp.where(segment_index == 0, fresh_batch, flow("zf_a")))
    rule("zr_m", lambda: returning[0])
    rule("zr_a", lambda: passed_along(flow("zr_m"), -1))
    next_back = deliver("D0", "G0_s", -1)
    rule("ag", lambda: retreat(flow("zr_a"), next_back()))
    rule("up", lambda: jnp.where(segment_index == segment_count - 1, fresh_cotangent, flow("ag")))

    spread("A3", lambda: flow("feed"))
    second_pre = product("F2", "A3")
    rule("out2", lambda: advance(flow("feed"), second_pre()))
    rule("sc2", lambda: scale(flow("up"), second_back()))
    back("G1", "sc2")
    last_back = deliver("D1", "G1_s")
    rule("gr2", lambda: retreat(flow("up"), last_back()))

    layer_outputs = jnp.stack([flow("out1"), flow("out2")], axis=0)[None]
    input_grads = jnp.stack([flow("gr1"), flow("gr2")], axis=0)[None]
    return (layer_outputs, input_grads)


def solution(mesh):
    in_specs = (
        P("segment", "row", "col"),
        P("segment", "col"),
        P("segment", "row", "col"),
        P("row", "col"),
        P("segment", "row", "col"),
        P("row", "col"),
        P("segment", None, "row", "col"),
    )
    out_specs = (P("segment", None, "row", "col"), P("segment", None, "row", "col"))
    return jax.shard_map(shards, mesh=mesh, in_specs=in_specs, out_specs=out_specs, check_vma=False)
```

```python
import jax
import jax.numpy as jnp
from jax import lax
from jax.sharding import PartitionSpec as P

F32 = jnp.float32
BF16 = jnp.bfloat16

TURNED = ("B0", "G0")
AT_ONCE = ("A0", "A1", "G0")
GATES = {
    "A0_o": ("weight",),
    "A1_a0": ("A0_x",),
    "A1_in": ("A0_m0",),
    "A1_s": ("B0_m0",),
    "A2_a0": ("A1_a1", "B0_m1"),
    "A2_in": ("B0_m0",),
    "A2_o": ("A2_a0",),
    "A2_s": ("B0_m1",),
    "A3_a0": ("A3_m1",),
    "A3_a1": ("sc2",),
    "A3_in": ("zf_a",),
    "B0_a0": ("F1_t0",),
    "B0_a1": ("F1_m1",),
    "B1_a0": ("G0_h",),
    "B1_a1": ("G0_s",),
    "B1_x": ("out1",),
    "D0_a0": ("feed",),
    "F1_a1": ("sc1",),
    "F1_m0": ("weight",),
    "F2_a0": ("G1_m1",),
    "F2_a1": ("G1_s",),
    "F2_x": ("A3_o",),
    "G0_a0": ("out1",),
    "G0_a1": ("B1_t0",),
    "G0_h": ("B1_t0", "feed"),
    "G1_a0": ("F2_t0",),
    "G1_a1": ("F2_m1",),
    "G1_h": ("G1_m1",),
    "G1_o": ("zt_a",),
    "out2": ("G1_m1",),
    "zr_a": ("F1_m1",),
    "zr_m": ("B0_m1",),
    "zt_m": ("F2_m1",),
}


def silu_slope(values):
    sigma = jax.nn.sigmoid(values)
    return sigma * (1.0 + values * (1.0 - sigma))


def passed_along(value, steps):
    count = lax.axis_size("segment")
    first, last = (max(0, -steps), min(count, count - steps))
    return lax.ppermute(value, "segment", [(source, source + steps) for source in range(first, last)])


def fixed(value):
    return lax.optimization_barrier(value)


def bits_of(count):
    return count.bit_length() - 1


def cut(value, count, axis=0):
    return jnp.split(value, count, axis=axis)


def xor_order(blocks, index):
    for bit in range(bits_of(len(blocks))):
        flip = 1 << bit
        is_set = (index & flip) != 0
        blocks = [jnp.where(is_set, blocks[k ^ flip], blocks[k]) for k in range(len(blocks))]
    return blocks


def col_swap(value, flip):
    count = lax.axis_size("col")
    return lax.ppermute(value, "col", [(source, source ^ flip) for source in range(count)])


class Plane:
    def __init__(self):
        self.rows, self.cols = lax.axis_size("row"), lax.axis_size("col")
        self.row, self.col = lax.axis_index("row"), lax.axis_index("col")
        self.steps = bits_of(self.rows)
        self.per_col = self.rows // self.cols
        self.home = self.row // self.per_col

    def flips(self, col, turn):
        return [1 << ((col + turn + step) % self.steps) for step in range(self.steps)]

    def places(self, col, turn):
        flips = self.flips(col, turn)
        return [
            sum(flip for at, flip in enumerate(flips) if place >> (self.steps - 1 - at) & 1)
            for place in range(self.rows)
        ]

    def choose(self, orders):
        chosen = orders[0]
        for at in range(1, len(orders)):
            picked = self.col % len(orders) == at
            chosen = [
                old if old is new else jnp.where(picked, new, old)
                for old, new in zip(chosen, orders[at])
            ]
        return chosen

    def by_place(self, blocks, turn):
        kinds = range(max(self.steps, 1))
        return self.choose([[blocks[k] for k in self.places(col, turn)] for col in kinds])

    def by_k(self, blocks, turn):
        orders = []
        for col in range(max(self.steps, 1)):
            places = self.places(col, turn)
            orders.append([blocks[places.index(k)] for k in range(self.rows)])
        return self.choose(orders)

    def step_swap(self, value, step, turn):
        pairs = []
        for row in range(self.rows):
            for col in range(self.cols):
                other = row ^ self.flips(col, turn)[step]
                pairs.append((row * self.cols + col, other * self.cols + col))
        return lax.ppermute(value, ("row", "col"), pairs)

    def across(self, value, shift, onward=0, only=None):
        pairs = []
        for row in range(self.rows):
            home = row // self.per_col
            for j in range(self.cols):
                other = row ^ (j * self.per_col + shift)
                pairs.append((row * self.cols + (home ^ j), other * self.cols + home))
        if not onward and only is None:
            return lax.ppermute(value, ("row", "col"), pairs)
        sections, size = lax.axis_size("segment"), self.rows * self.cols
        pairs = [
            (at * size + source, (at + onward) * size + target)
            for at in range(sections)
            if 0 <= at + onward < sections and only in (None, at)
            for source, target in pairs
        ]
        return lax.ppermute(value, ("segment", "row", "col"), pairs)

    def joined(self, half, others, at_once):
        if at_once:
            halves = xor_order(others, self.home)
        else:
            halves = xor_order([half] + others, self.col ^ self.home)
        return [block for half in halves for block in cut(half, self.per_col)]

    def shares(self, partial, turn):
        ordered = jnp.concatenate(self.by_k(cut(partial, self.rows), turn), axis=0)
        return xor_order(cut(ordered, self.cols), self.col ^ self.home)

    def in_columns(self, arrived):
        return jnp.concatenate(xor_order(arrived, self.row % self.per_col), axis=1)


class Flow:
    def __init__(self, gates):
        self.gates, self.rules, self.values = gates, {}, {}

    def rule(self, name, make):
        self.rules[name] = make

    def __call__(self, name):
        if name not in self.values:
            value = self.rules[name]()
            others = [self(other) for other in self.gates.get(name, ()) if other in self.rules]
            if others:
                value = lax.optimization_barrier((value, others))[0]
            self.values[name] = value
        return self.values[name]


def shards(weights, layer_gains, incoming, fresh_batch, returning, fresh_cotangent, stashed_inputs):
    segment_index = lax.axis_index("segment")
    segment_count = lax.axis_size("segment")
    layer_gain = layer_gains[0][None, :]
    plane = Plane()
    steps, shifts = plane.steps, range(plane.per_col)
    flow = Flow(GATES)
    rule = flow.rule

    def advance(own_block, pre_act):
        return fixed((own_block.astype(F32) + layer_gain * jax.nn.silu(pre_act)).astype(BF16))

    def scale(upstream, pre_act):
        return fixed((upstream.astype(F32) * layer_gain * silu_slope(pre_act)).astype(BF16))

    def retreat(upstream, back_term):
        return (upstream.astype(F32) + back_term.astype(F32)).astype(BF16)

    def spread(name, block):
        def message(shift):
            pieces = cut(flow(f"{name}_in"), plane.per_col, axis=1)
            return xor_order(pieces, plane.row % plane.per_col)[shift]

        def others():
            half = flow(f"{name}_s")
            if name in AT_ONCE:
                halves = lax.all_gather(half, "col", axis=0, tiled=False)
                return [halves[col] for col in range(plane.cols)]
            return [col_swap(half, flip) for flip in range(1, plane.cols)]

        rule(f"{name}_in", block)
        for shift in shifts:
            rule(f"{name}_m{shift}", lambda shift=shift: message(shift))
            rule(f"{name}_a{shift}", lambda shift=shift: plane.across(flow(f"{name}_m{shift}"), shift))
        rule(f"{name}_s", lambda: jnp.concatenate([flow(f"{name}_a{at}") for at in shifts], axis=0))
        rule(f"{name}_o", others)
        rule(f"{name}_x", lambda: plane.joined(flow(f"{name}_s"), flow(f"{name}_o"), name in AT_ONCE))

    def product(name, source):
        turn = int(name in TURNED)

        def multiplied():
            full = jnp.concatenate(plane.by_place(flow(f"{name}_x"), turn), axis=0)
            return jnp.dot(full, flow("weight"), preferred_element_type=F32).astype(BF16)

        def message(step):
            return fixed(cut(flow(f"{name}_t{step}"), 2)[1].astype(BF16))

        def total(step):
            ours = cut(flow(f"{name}_t{step}"), 2)[0]
            return ours.astype(F32) + flow(f"{name}_a{step}").astype(F32)

        rule(f"{name}_x", lambda: flow(f"{source}_x"))
        rule(f"{name}_t0", multiplied)
        for step in range(steps):
            rule(f"{name}_m{step}", lambda step=step: message(step))
            rule(
                f"{name}_a{step}",
                lambda step=step: plane.step_swap(flow(f"{name}_m{step}"), step, turn),
            )
            rule(f"{name}_t{step + 1}", lambda step=step: total(step))
        return lambda: flow(f"{name}_t{steps}").astype(F32)

    def back(name, scaled):
        turn = int(name in TURNED)

        def doubled(at):
            block = jnp.concatenate([flow(f"{name}_m{at}"), flow(f"{name}_a{at}")], axis=0)
            return fixed(block) if at + 1 < steps else block

        def multiplied():
            return lax.dot_general(
                flow(f"{name}_m{steps}"),
                flow("weight"),
                (((1,), (1,)), ((), ())),
                preferred_element_type=F32,
            ).astype(BF16)

        def others():
            shares = flow(f"{name}_h")
            if name in AT_ONCE and plane.cols == 2:
                both = lax.all_gather(shares[1], "col", axis=0, tiled=False)
                return [jnp.where(plane.col == 0, both[1], both[0])]
            return [col_swap(shares[flip], flip) for flip in range(1, plane.cols)]

        def total():
            ours = flow(f"{name}_h")[0].astype(F32)
            return fixed(sum([o.astype(F32) for o in flow(f"{name}_o")], ours).astype(BF16))

        rule(f"{name}_m0", lambda: flow(scaled))
        for at in range(steps):
            step = steps - 1 - at
            rule(
                f"{name}_a{at}",
                lambda at=at, step=step: plane.step_swap(flow(f"{name}_m{at}"), step, turn),
            )
            rule(f"{name}_m{at + 1}", lambda at=at: doubled(at))
        rule(f"{name}_p", multiplied)
        rule(f"{name}_h", lambda: fixed(plane.shares(flow(f"{name}_p"), turn)))
        rule(f"{name}_o", others)
        rule(f"{name}_s", total)

    def deliver(name, source, onward=0, only=None):
        rule(f"{name}_m", lambda: cut(flow(source), plane.per_col))
        for shift in shifts:
            rule(
                f"{name}_a{shift}",
                lambda shift=shift: plane.across(flow(f"{name}_m")[shift], shift, onward, only),
            )
        return lambda: plane.in_columns([flow(f"{name}_a{shift}") for shift in shifts])

    rule("weight", lambda: weights[0])

    spread("A0", lambda: stashed_inputs[0, 0])
    spread("A1", lambda: incoming[0])
    spread("A2", lambda: stashed_inputs[0, 1])
    first_back, first_pre, second_back = product("B0", "A0"), product("F1", "A1"), product("B1", "A2")
    rule("sc1", lambda: scale(returning[0], first_back()))
    rule("out1", lambda: advance(incoming[0], first_pre()))
    back("G0", "sc1")

    rule("zf_a", lambda: passed_along(flow("out1"), 1))
    rule("feed", lambda: jnp.where(segment_index == 0, fresh_batch, flow("zf_a")))
    rule("zr_m", lambda: returning[0])
    rule("zr_a", lambda: passed_along(flow("zr_m"), -1))
    next_back = deliver("D0", "G0_s", -1)
    rule("ag", lambda: retreat(flow("zr_a"), next_back()))
    own_back = deliver("W0", "G0_s", 0, 0)
    rule("zt_m", lambda: flow("ag"))
    rule("zt_a", lambda: passed_along(flow("zt_m"), 1))
    rule("gw", lambda: fixed(retreat(returning[0], own_back())))
    rule("gr1", lambda: jnp.where(segment_index == 0, flow("gw"), flow("zt_a")))
    rule("up", lambda: jnp.where(segment_index == segment_count - 1, fresh_cotangent, flow("ag")))

    spread("A3", lambda: flow("feed"))
    second_pre = product("F2", "A3")
    rule("out2", lambda: advance(flow("feed"), second_pre()))
    rule("sc2", lambda: scale(flow("up"), second_back()))
    back("G1", "sc2")
    last_back = deliver("D1", "G1_s")
    rule("gr2", lambda: retreat(flow("up"), last_back()))

    layer_outputs = jnp.stack([flow("out1"), flow("out2")], axis=0)[None]
    input_grads = jnp.stack([flow("gr1"), flow("gr2")], axis=0)[None]
    return (layer_outputs, input_grads)


def solution(mesh):
    in_specs = (
        P("segment", "row", "col"),
        P("segment", "col"),
        P("segment", "row", "col"),
        P("row", "col"),
        P("segment", "row", "col"),
        P("row", "col"),
        P("segment", None, "row", "col"),
    )
    out_specs = (P("segment", None, "row", "col"), P("segment", None, "row", "col"))
    return jax.shard_map(shards, mesh=mesh, in_specs=in_specs, out_specs=out_specs, check_vma=False)
```

```python
import jax
import jax.numpy as jnp
from jax import lax
from jax.sharding import PartitionSpec as P

F32 = jnp.float32
BF16 = jnp.bfloat16

TURNED = ("B0", "G0")
AT_ONCE = ("A0", "A1", "G0")
GATES = {
    "A0_o": ("weight",),
    "A1_a0": ("A0_x",),
    "A1_in": ("A0_m0",),
    "A1_s": ("B0_m0",),
    "A2_a0": ("A1_a1", "B0_m1"),
    "A2_in": ("B0_m0",),
    "A2_o": ("A2_a0",),
    "A2_s": ("B0_m1",),
    "A3_a0": ("A3_m1",),
    "A3_a1": ("sc2",),
    "A3_in": ("zf_a",),
    "B0_a0": ("F1_t0",),
    "B0_a1": ("F1_m1",),
    "B1_a0": ("G0_h",),
    "B1_a1": ("G0_s",),
    "B1_x": ("out1",),
    "D0_a0": ("feed",),
    "F1_a1": ("sc1",),
    "F1_m0": ("weight",),
    "F2_a0": ("G1_m1",),
    "F2_a1": ("G1_s",),
    "F2_x": ("A3_o",),
    "G0_a0": ("out1",),
    "G0_a1": ("B1_t0",),
    "G0_h": ("B1_t0", "feed"),
    "G1_a0": ("F2_t0",),
    "G1_a1": ("F2_m1",),
    "G1_h": ("G1_m1",),
    "G1_o": ("zt_a",),
    "out2": ("G1_m1",),
    "zr_a": ("F1_m1",),
    "zr_m": ("B0_m1",),
    "zt_m": ("F2_m1",),
}


def silu_slope(values):
    sigma = jax.nn.sigmoid(values)
    return sigma * (1.0 + values * (1.0 - sigma))


def passed_along(value, steps):
    count = lax.axis_size("segment")
    first, last = (max(0, -steps), min(count, count - steps))
    return lax.ppermute(value, "segment", [(source, source + steps) for source in range(first, last)])


def fixed(value):
    return lax.optimization_barrier(value)


def bits_of(count):
    return count.bit_length() - 1


def cut(value, count, axis=0):
    return jnp.split(value, count, axis=axis)


def xor_order(blocks, index):
    for bit in range(bits_of(len(blocks))):
        flip = 1 << bit
        is_set = (index & flip) != 0
        blocks = [jnp.where(is_set, blocks[k ^ flip], blocks[k]) for k in range(len(blocks))]
    return blocks


def col_swap(value, flip):
    count = lax.axis_size("col")
    return lax.ppermute(value, "col", [(source, source ^ flip) for source in range(count)])


class Plane:
    def __init__(self):
        self.rows, self.cols = lax.axis_size("row"), lax.axis_size("col")
        self.row, self.col = lax.axis_index("row"), lax.axis_index("col")
        self.steps = bits_of(self.rows)
        self.per_col = self.rows // self.cols
        self.home = self.row // self.per_col

    def flips(self, col, turn):
        return [1 << ((col + turn + step) % self.steps) for step in range(self.steps)]

    def places(self, col, turn):
        flips = self.flips(col, turn)
        return [
            sum(flip for at, flip in enumerate(flips) if place >> (self.steps - 1 - at) & 1)
            for place in range(self.rows)
        ]

    def choose(self, orders):
        chosen = orders[0]
        for at in range(1, len(orders)):
            picked = self.col % len(orders) == at
            chosen = [
                old if old is new else jnp.where(picked, new, old)
                for old, new in zip(chosen, orders[at])
            ]
        return chosen

    def by_place(self, blocks, turn):
        kinds = range(max(self.steps, 1))
        return self.choose([[blocks[k] for k in self.places(col, turn)] for col in kinds])

    def by_k(self, blocks, turn):
        orders = []
        for col in range(max(self.steps, 1)):
            places = self.places(col, turn)
            orders.append([blocks[places.index(k)] for k in range(self.rows)])
        return self.choose(orders)

    def step_swap(self, value, step, turn):
        pairs = []
        for row in range(self.rows):
            for col in range(self.cols):
                other = row ^ self.flips(col, turn)[step]
                pairs.append((row * self.cols + col, other * self.cols + col))
        return lax.ppermute(value, ("row", "col"), pairs)

    def across(self, value, shift, onward=0, only=None):
        pairs = []
        for row in range(self.rows):
            home = row // self.per_col
            for j in range(self.cols):
                other = row ^ (j * self.per_col + shift)
                pairs.append((row * self.cols + (home ^ j), other * self.cols + home))
        if not onward and only is None:
            return lax.ppermute(value, ("row", "col"), pairs)
        sections, size = lax.axis_size("segment"), self.rows * self.cols
        pairs = [
            (at * size + source, (at + onward) * size + target)
            for at in range(sections)
            if 0 <= at + onward < sections and only in (None, at)
            for source, target in pairs
        ]
        return lax.ppermute(value, ("segment", "row", "col"), pairs)

    def joined(self, half, others, at_once):
        if at_once:
            halves = xor_order(others, self.home)
        else:
            halves = xor_order([half] + others, self.col ^ self.home)
        return [block for half in halves for block in cut(half, self.per_col)]

    def shares(self, partial, turn):
        ordered = jnp.concatenate(self.by_k(cut(partial, self.rows), turn), axis=0)
        return xor_order(cut(ordered, self.cols), self.col ^ self.home)

    def in_columns(self, arrived):
        return jnp.concatenate(xor_order(arrived, self.row % self.per_col), axis=1)


class Flow:
    def __init__(self, gates):
        self.gates, self.rules, self.values = gates, {}, {}

    def rule(self, name, make):
        self.rules[name] = make

    def __call__(self, name):
        if name not in self.values:
            value = self.rules[name]()
            others = [self(other) for other in self.gates.get(name, ()) if other in self.rules]
            if others:
                value = lax.optimization_barrier((value, others))[0]
            self.values[name] = value
        return self.values[name]


def shards(weights, layer_gains, incoming, fresh_batch, returning, fresh_cotangent, stashed_inputs):
    segment_index = lax.axis_index("segment")
    segment_count = lax.axis_size("segment")
    layer_gain = layer_gains[0][None, :]
    plane = Plane()
    steps, shifts = plane.steps, range(plane.per_col)
    flow = Flow(GATES)
    rule = flow.rule

    def advance(own_block, pre_act):
        return fixed((own_block.astype(F32) + layer_gain * jax.nn.silu(pre_act)).astype(BF16))

    def scale(upstream, pre_act):
        return fixed((upstream.astype(F32) * layer_gain * silu_slope(pre_act)).astype(BF16))

    def retreat(upstream, back_term):
        return (upstream.astype(F32) + back_term.astype(F32)).astype(BF16)

    def spread(name, block):
        def message(shift):
            pieces = cut(flow(f"{name}_in"), plane.per_col, axis=1)
            return xor_order(pieces, plane.row % plane.per_col)[shift]

        def others():
            half = flow(f"{name}_s")
            if name in AT_ONCE:
                halves = lax.all_gather(half, "col", axis=0, tiled=False)
                return [halves[col] for col in range(plane.cols)]
            return [col_swap(half, flip) for flip in range(1, plane.cols)]

        rule(f"{name}_in", block)
        for shift in shifts:
            rule(f"{name}_m{shift}", lambda shift=shift: message(shift))
            rule(f"{name}_a{shift}", lambda shift=shift: plane.across(flow(f"{name}_m{shift}"), shift))
        rule(f"{name}_s", lambda: jnp.concatenate([flow(f"{name}_a{at}") for at in shifts], axis=0))
        rule(f"{name}_o", others)
        rule(f"{name}_x", lambda: plane.joined(flow(f"{name}_s"), flow(f"{name}_o"), name in AT_ONCE))

    def product(name, source):
        turn = int(name in TURNED)

        def multiplied():
            full = jnp.concatenate(plane.by_place(flow(f"{name}_x"), turn), axis=0)
            return jnp.dot(full, flow("weight"), preferred_element_type=F32).astype(BF16)

        def message(step):
            return fixed(cut(flow(f"{name}_t{step}"), 2)[1].astype(BF16))

        def total(step):
            ours = cut(flow(f"{name}_t{step}"), 2)[0]
            return ours.astype(F32) + flow(f"{name}_a{step}").astype(F32)

        rule(f"{name}_x", lambda: flow(f"{source}_x"))
        rule(f"{name}_t0", multiplied)
        for step in range(steps):
            rule(f"{name}_m{step}", lambda step=step: message(step))
            rule(
                f"{name}_a{step}",
                lambda step=step: plane.step_swap(flow(f"{name}_m{step}"), step, turn),
            )
            rule(f"{name}_t{step + 1}", lambda step=step: total(step))
        return lambda: flow(f"{name}_t{steps}").astype(F32)

    def back(name, scaled):
        turn = int(name in TURNED)

        def doubled(at):
            block = jnp.concatenate([flow(f"{name}_m{at}"), flow(f"{name}_a{at}")], axis=0)
            return fixed(block) if at + 1 < steps else block

        def multiplied():
            return lax.dot_general(
                flow(f"{name}_m{steps}"),
                flow("weight"),
                (((1,), (1,)), ((), ())),
                preferred_element_type=F32,
            ).astype(BF16)

        def others():
            shares = flow(f"{name}_h")
            if name in AT_ONCE and plane.cols == 2:
                both = lax.all_gather(shares[1], "col", axis=0, tiled=False)
                return [jnp.where(plane.col == 0, both[1], both[0])]
            return [col_swap(shares[flip], flip) for flip in range(1, plane.cols)]

        def total():
            ours = flow(f"{name}_h")[0].astype(F32)
            return fixed(sum([o.astype(F32) for o in flow(f"{name}_o")], ours).astype(BF16))

        rule(f"{name}_m0", lambda: flow(scaled))
        for at in range(steps):
            step = steps - 1 - at
            rule(
                f"{name}_a{at}",
                lambda at=at, step=step: plane.step_swap(flow(f"{name}_m{at}"), step, turn),
            )
            rule(f"{name}_m{at + 1}", lambda at=at: doubled(at))
        rule(f"{name}_p", multiplied)
        rule(f"{name}_h", lambda: fixed(plane.shares(flow(f"{name}_p"), turn)))
        rule(f"{name}_o", others)
        rule(f"{name}_s", total)

    def deliver(name, source, onward=0, only=None):
        rule(f"{name}_m", lambda: cut(flow(source), plane.per_col))
        for shift in shifts:
            rule(
                f"{name}_a{shift}",
                lambda shift=shift: plane.across(flow(f"{name}_m")[shift], shift, onward, only),
            )
        return lambda: plane.in_columns([flow(f"{name}_a{shift}") for shift in shifts])

    rule("weight", lambda: weights[0])

    spread("A0", lambda: stashed_inputs[0, 0])
    spread("A1", lambda: incoming[0])
    spread("A2", lambda: stashed_inputs[0, 1])
    first_back, first_pre, second_back = product("B0", "A0"), product("F1", "A1"), product("B1", "A2")
    rule("sc1", lambda: scale(returning[0], first_back()))
    rule("out1", lambda: advance(incoming[0], first_pre()))
    back("G0", "sc1")

    rule("zf_a", lambda: passed_along(flow("out1"), 1))
    rule("feed", lambda: jnp.where(segment_index == 0, fresh_batch, flow("zf_a")))
    rule("zr_m", lambda: returning[0])
    rule("zr_a", lambda: passed_along(flow("zr_m"), -1))
    next_back = deliver("D0", "G0_s", -1)
    rule("ag", lambda: retreat(flow("zr_a"), next_back()))
    own_back = deliver("W0", "G0_s", 0, 0)
    rule("zt_m", lambda: flow("ag"))
    rule("zt_a", lambda: passed_along(flow("zt_m"), 1))
    rule("gw", lambda: fixed(retreat(returning[0], own_back())))
    rule("gr1", lambda: jnp.where(segment_index == 0, flow("gw"), flow("zt_a")))
    rule("up", lambda: jnp.where(segment_index == segment_count - 1, fresh_cotangent, flow("ag")))

    spread("A3", lambda: flow("feed"))
    second_pre = product("F2", "A3")
    rule("out2", lambda: advance(flow("feed"), second_pre()))
    rule("sc2", lambda: scale(flow("up"), second_back()))
    back("G1", "sc2")
    last_back = deliver("D1", "G1_s")
    rule("gr2", lambda: retreat(flow("up"), last_back()))

    layer_outputs = jnp.stack([flow("out1"), flow("out2")], axis=0)[None]
    first_half = fixed(jnp.stack([flow("gr1"), flow("up")], axis=0))
    input_grads = lax.dynamic_update_index_in_dim(first_half, flow("gr2"), 1, 0)[None]
    return (layer_outputs, input_grads)


def solution(mesh):
    in_specs = (
        P("segment", "row", "col"),
        P("segment", "col"),
        P("segment", "row", "col"),
        P("row", "col"),
        P("segment", "row", "col"),
        P("row", "col"),
        P("segment", None, "row", "col"),
    )
    out_specs = (P("segment", None, "row", "col"), P("segment", None, "row", "col"))
    return jax.shard_map(shards, mesh=mesh, in_specs=in_specs, out_specs=out_specs, check_vma=False)
```

```python
import jax
import jax.numpy as jnp
from jax import lax
from jax.sharding import PartitionSpec as P

F32 = jnp.float32
BF16 = jnp.bfloat16

TURNED = ("B0", "G0")
AT_ONCE = ("A0", "A1", "G0")
GATES = {
    "A0_o": ("weight",),
    "A1_a0": ("A0_x",),
    "A1_in": ("A0_m0",),
    "A1_s": ("B0_m0",),
    "A2_a0": ("A1_a1", "B0_m1"),
    "A2_in": ("B0_m0",),
    "A2_o": ("A2_a0",),
    "A2_s": ("B0_m1",),
    "A3_a0": ("A3_m1",),
    "A3_a1": ("sc2",),
    "A3_in": ("zf_a",),
    "B0_a0": ("F1_t0",),
    "B0_a1": ("F1_m1",),
    "B1_a0": ("G0_h",),
    "B1_a1": ("G0_s",),
    "B1_x": ("out1",),
    "D0_a0": ("feed",),
    "F1_a1": ("sc1",),
    "F1_m0": ("weight",),
    "F2_a0": ("G1_m1",),
    "F2_a1": ("G1_s",),
    "F2_x": ("A3_o",),
    "G0_a0": ("out1",),
    "G0_a1": ("B1_t0",),
    "G0_h": ("B1_t0", "feed"),
    "G1_a0": ("F2_t0",),
    "G1_a1": ("F2_m1",),
    "G1_h": ("G1_m1",),
    "G1_o": ("zt_a",),
    "out2": ("G1_m1",),
    "zr_a": ("F1_m1",),
    "zr_m": ("B0_m1",),
    "zt_m": ("F2_m1",),
}


def silu_slope(values):
    sigma = jax.nn.sigmoid(values)
    return sigma * (1.0 + values * (1.0 - sigma))


def passed_along(value, steps):
    count = lax.axis_size("segment")
    first, last = (max(0, -steps), min(count, count - steps))
    return lax.ppermute(value, "segment", [(source, source + steps) for source in range(first, last)])


def fixed(value):
    return lax.optimization_barrier(value)


def bits_of(count):
    return count.bit_length() - 1


def cut(value, count, axis=0):
    return jnp.split(value, count, axis=axis)


def xor_order(blocks, index):
    for bit in range(bits_of(len(blocks))):
        flip = 1 << bit
        is_set = (index & flip) != 0
        blocks = [jnp.where(is_set, blocks[k ^ flip], blocks[k]) for k in range(len(blocks))]
    return blocks


def col_swap(value, flip):
    count = lax.axis_size("col")
    return lax.ppermute(value, "col", [(source, source ^ flip) for source in range(count)])


class Plane:
    def __init__(self):
        self.rows, self.cols = lax.axis_size("row"), lax.axis_size("col")
        self.row, self.col = lax.axis_index("row"), lax.axis_index("col")
        self.steps = bits_of(self.rows)
        self.per_col = self.rows // self.cols
        self.home = self.row // self.per_col

    def flips(self, col, turn):
        return [1 << ((col + turn + step) % self.steps) for step in range(self.steps)]

    def places(self, col, turn):
        flips = self.flips(col, turn)
        return [
            sum(flip for at, flip in enumerate(flips) if place >> (self.steps - 1 - at) & 1)
            for place in range(self.rows)
        ]

    def choose(self, orders):
        chosen = orders[0]
        for at in range(1, len(orders)):
            picked = self.col % len(orders) == at
            chosen = [
                old if old is new else jnp.where(picked, new, old)
                for old, new in zip(chosen, orders[at])
            ]
        return chosen

    def by_place(self, blocks, turn):
        kinds = range(max(self.steps, 1))
        return self.choose([[blocks[k] for k in self.places(col, turn)] for col in kinds])

    def by_k(self, blocks, turn):
        orders = []
        for col in range(max(self.steps, 1)):
            places = self.places(col, turn)
            orders.append([blocks[places.index(k)] for k in range(self.rows)])
        return self.choose(orders)

    def step_swap(self, value, step, turn):
        pairs = []
        for row in range(self.rows):
            for col in range(self.cols):
                other = row ^ self.flips(col, turn)[step]
                pairs.append((row * self.cols + col, other * self.cols + col))
        return lax.ppermute(value, ("row", "col"), pairs)

    def across(self, value, shift, onward=0, only=None):
        pairs = []
        for row in range(self.rows):
            home = row // self.per_col
            for j in range(self.cols):
                other = row ^ (j * self.per_col + shift)
                pairs.append((row * self.cols + (home ^ j), other * self.cols + home))
        if not onward and only is None:
            return lax.ppermute(value, ("row", "col"), pairs)
        sections, size = lax.axis_size("segment"), self.rows * self.cols
        pairs = [
            (at * size + source, (at + onward) * size + target)
            for at in range(sections)
            if 0 <= at + onward < sections and only in (None, at)
            for source, target in pairs
        ]
        return lax.ppermute(value, ("segment", "row", "col"), pairs)

    def joined(self, half, others, at_once):
        if at_once:
            halves = xor_order(others, self.home)
        else:
            halves = xor_order([half] + others, self.col ^ self.home)
        return [block for half in halves for block in cut(half, self.per_col)]

    def shares(self, partial, turn):
        ordered = jnp.concatenate(self.by_k(cut(partial, self.rows), turn), axis=0)
        return xor_order(cut(ordered, self.cols), self.col ^ self.home)

    def in_columns(self, arrived):
        return jnp.concatenate(xor_order(arrived, self.row % self.per_col), axis=1)


class Flow:
    def __init__(self, gates):
        self.gates, self.rules, self.values = gates, {}, {}

    def rule(self, name, make):
        self.rules[name] = make

    def __call__(self, name):
        if name not in self.values:
            value = self.rules[name]()
            others = [self(other) for other in self.gates.get(name, ()) if other in self.rules]
            if others:
                value = lax.optimization_barrier((value, others))[0]
            self.values[name] = value
        return self.values[name]


def shards(weights, layer_gains, incoming, fresh_batch, returning, fresh_cotangent, stashed_inputs):
    segment_index = lax.axis_index("segment")
    segment_count = lax.axis_size("segment")
    layer_gain = layer_gains[0][None, :]
    plane = Plane()
    steps, shifts = plane.steps, range(plane.per_col)
    flow = Flow(GATES)
    rule = flow.rule

    def advance(own_block, pre_act):
        return fixed((own_block.astype(F32) + layer_gain * jax.nn.silu(pre_act)).astype(BF16))

    def scale(upstream, pre_act):
        return fixed((upstream.astype(F32) * layer_gain * silu_slope(pre_act)).astype(BF16))

    def retreat(upstream, back_term):
        return (upstream.astype(F32) + back_term.astype(F32)).astype(BF16)

    def spread(name, block):
        def message(shift):
            pieces = cut(flow(f"{name}_in"), plane.per_col, axis=1)
            return xor_order(pieces, plane.row % plane.per_col)[shift]

        def others():
            half = flow(f"{name}_s")
            if name in AT_ONCE:
                halves = lax.all_gather(half, "col", axis=0, tiled=False)
                return [halves[col] for col in range(plane.cols)]
            return [col_swap(half, flip) for flip in range(1, plane.cols)]

        rule(f"{name}_in", block)
        for shift in shifts:
            rule(f"{name}_m{shift}", lambda shift=shift: message(shift))
            rule(f"{name}_a{shift}", lambda shift=shift: plane.across(flow(f"{name}_m{shift}"), shift))
        rule(f"{name}_s", lambda: jnp.concatenate([flow(f"{name}_a{at}") for at in shifts], axis=0))
        rule(f"{name}_o", others)
        rule(f"{name}_x", lambda: plane.joined(flow(f"{name}_s"), flow(f"{name}_o"), name in AT_ONCE))

    def product(name, source):
        turn = int(name in TURNED)

        def multiplied():
            full = jnp.concatenate(plane.by_place(flow(f"{name}_x"), turn), axis=0)
            return jnp.dot(full, flow("weight"), preferred_element_type=F32).astype(BF16)

        def message(step):
            return fixed(cut(flow(f"{name}_t{step}"), 2)[1].astype(BF16))

        def total(step):
            ours = cut(flow(f"{name}_t{step}"), 2)[0]
            return ours.astype(F32) + flow(f"{name}_a{step}").astype(F32)

        rule(f"{name}_x", lambda: flow(f"{source}_x"))
        rule(f"{name}_t0", multiplied)
        for step in range(steps):
            rule(f"{name}_m{step}", lambda step=step: message(step))
            rule(
                f"{name}_a{step}",
                lambda step=step: plane.step_swap(flow(f"{name}_m{step}"), step, turn),
            )
            rule(f"{name}_t{step + 1}", lambda step=step: total(step))
        return lambda: flow(f"{name}_t{steps}").astype(F32)

    def back(name, scaled):
        turn = int(name in TURNED)

        def doubled(at):
            block = jnp.concatenate([flow(f"{name}_m{at}"), flow(f"{name}_a{at}")], axis=0)
            return fixed(block) if at + 1 < steps else block

        def multiplied():
            return lax.dot_general(
                flow(f"{name}_m{steps}"),
                flow("weight"),
                (((1,), (1,)), ((), ())),
                preferred_element_type=F32,
            ).astype(BF16)

        def others():
            shares = flow(f"{name}_h")
            if name in AT_ONCE and plane.cols == 2:
                both = lax.all_gather(shares[1], "col", axis=0, tiled=False)
                return [jnp.where(plane.col == 0, both[1], both[0])]
            return [col_swap(shares[flip], flip) for flip in range(1, plane.cols)]

        def total():
            ours = flow(f"{name}_h")[0].astype(F32)
            return fixed(sum([o.astype(F32) for o in flow(f"{name}_o")], ours).astype(BF16))

        rule(f"{name}_m0", lambda: flow(scaled))
        for at in range(steps):
            step = steps - 1 - at
            rule(
                f"{name}_a{at}",
                lambda at=at, step=step: plane.step_swap(flow(f"{name}_m{at}"), step, turn),
            )
            rule(f"{name}_m{at + 1}", lambda at=at: doubled(at))
        rule(f"{name}_p", multiplied)
        rule(f"{name}_h", lambda: fixed(plane.shares(flow(f"{name}_p"), turn)))
        rule(f"{name}_o", others)
        rule(f"{name}_s", total)

    def deliver(name, source, onward=0, only=None):
        rule(f"{name}_m", lambda: cut(flow(source), plane.per_col))
        for shift in shifts:
            rule(
                f"{name}_a{shift}",
                lambda shift=shift: plane.across(flow(f"{name}_m")[shift], shift, onward, only),
            )
        return lambda: plane.in_columns([flow(f"{name}_a{shift}") for shift in shifts])

    rule("weight", lambda: weights[0])

    spread("A0", lambda: stashed_inputs[0, 0])
    spread("A1", lambda: incoming[0])
    spread("A2", lambda: stashed_inputs[0, 1])
    first_back, first_pre, second_back = product("B0", "A0"), product("F1", "A1"), product("B1", "A2")
    rule("sc1", lambda: scale(returning[0], first_back()))
    rule("out1", lambda: advance(incoming[0], first_pre()))
    back("G0", "sc1")

    rule("zf_a", lambda: passed_along(flow("out1"), 1))
    rule("feed", lambda: jnp.where(segment_index == 0, fresh_batch, flow("zf_a")))
    rule("zr_m", lambda: returning[0])
    rule("zr_a", lambda: passed_along(flow("zr_m"), -1))
    next_back = deliver("D0", "G0_s", -1)
    rule("ag", lambda: retreat(flow("zr_a"), next_back()))
    own_back = deliver("W0", "G0_s", 0, 0)
    rule("zt_m", lambda: flow("ag"))
    rule("zt_a", lambda: passed_along(flow("zt_m"), 1))
    rule("gw", lambda: fixed(retreat(returning[0], own_back())))
    rule("gr1", lambda: jnp.where(segment_index == 0, flow("gw"), flow("zt_a")))
    rule("up", lambda: jnp.where(segment_index == segment_count - 1, fresh_cotangent, flow("ag")))

    spread("A3", lambda: flow("feed"))
    second_pre = product("F2", "A3")
    rule("out2", lambda: advance(flow("feed"), second_pre()))
    rule("sc2", lambda: scale(flow("up"), second_back()))
    back("G1", "sc2")
    last_back = deliver("D1", "G1_s")
    rule("gr2", lambda: retreat(flow("up"), last_back()))

    first_outputs = fixed(jnp.stack([flow("out1"), flow("feed")], axis=0))
    layer_outputs = lax.dynamic_update_index_in_dim(first_outputs, flow("out2"), 1, 0)[None]
    first_half = fixed(jnp.stack([flow("gr1"), flow("up")], axis=0))
    input_grads = lax.dynamic_update_index_in_dim(first_half, flow("gr2"), 1, 0)[None]
    return (layer_outputs, input_grads)


def solution(mesh):
    in_specs = (
        P("segment", "row", "col"),
        P("segment", "col"),
        P("segment", "row", "col"),
        P("row", "col"),
        P("segment", "row", "col"),
        P("row", "col"),
        P("segment", None, "row", "col"),
    )
    out_specs = (P("segment", None, "row", "col"), P("segment", None, "row", "col"))
    return jax.shard_map(shards, mesh=mesh, in_specs=in_specs, out_specs=out_specs, check_vma=False)
```
